32 devices in a mesh: row: 4 (over z), col: 8 (over y, x, core).
Axes of the slice: x: 2, y: 2, z: 4, core: 2. Of those that a mesh axis runs over, the one named last changes fastest.
Arguments:
- tile_u: bfloat16 [32, 8, 2048, 128], P('row', 'col'), may hold values from -6 to 6
- tile_v: bfloat16 [32, 8, 2048, 128], P('row', 'col'), may hold values from -0.5 to 0.5
- tile_rank: int32 [32, 8], P('row', 'col'), may hold values from 16 to 128, as said below
- listed: int32 [32, 8], P('row', 'col'), may hold values from 0 to 1, as said below
- row_u: bfloat16 [32, 2048, 128], P('row', 'col'), may hold values from -6 to 6
- row_v: bfloat16 [32, 2048, 128], P('row', 'col'), may hold values from -0.5 to 0.5
- row_rank: int32 [32], P('row'), may hold values from 16 to 128
- col_u: bfloat16 [8, 2048, 128], P('col', 'row'), may hold values from -6 to 6
- col_v: bfloat16 [8, 2048, 128], P('col', 'row'), may hold values from -0.5 to 0.5
- col_rank: int32 [8], P('col'), may hold values from 16 to 112
- sketch: bfloat16 [2048, 128], replicated, may hold values from -0.125 to 0.125
Outputs:
- out_u: bfloat16 [32, 8, 2048, 128], P('row', 'col')
- out_v: bfloat16 [32, 8, 2048, 128], P('row', 'col')
The draws below stay inside these ranges and needn't reach their ends.
Inputs may be any that keep to these rules, and one draw needn't show every extreme that they name: A tile with listed 0 has tile_rank plus the col_rank of its column at most 128; a tile with listed 1 has more than 128. The tiles of one device are tile rows a * 8 to a * 8 + 7 and tile columns b * 1 to b + 1 - 1 for its indices a along row and b along col. Two devices of the same row index whose col indices differ by 4 hold together at most 8 listed tiles; some device holds 8.
All inputs are finite; a program needn't handle non-finite values.
Results may differ from the reference program's by a relative error of at most 0.0072.
Values may be sent and summed in bfloat16 or wider, within the bound.
No kernel may reach another device: no remote copies, remote signals or barrier semaphores. Data moves between devices by JAX's collectives and lax.ppermute only.
A program may use at most 192 MiB of HBM per device.

```python
import jax
import jax.numpy as jnp
from jax import lax

B = 2048
R = 128
S = 128
TR = 8
TC = 1
NTR = 32
NTC = 8
N_ROW = 4
N_COL = 8


def joint_ranks(key):
    base = jax.random.fold_in(key, 41)
    keys = jax.random.split(base, 7)
    col_rank = jax.random.randint(keys[0], (NTC,), R // 8, R - R // 8 + 1)
    capacity = TR * TC
    pairs = N_COL // 2
    first = jax.random.randint(keys[1], (N_ROW, pairs), 0, capacity + 1)
    corner = (lax.broadcasted_iota(jnp.int32, (N_ROW, pairs), 0) == 0) & (lax.broadcasted_iota(jnp.int32, (N_ROW, pairs), 1) == 0)
    first = jnp.where(corner, capacity, first)
    second = jax.random.randint(keys[2], (N_ROW, pairs), 0, capacity - first + 1)
    flipped = jax.random.randint(keys[3], (N_ROW, pairs), 0, 2)
    lower_half = jnp.where(flipped == 1, second, first)
    upper_half = jnp.where(flipped == 1, first, second)
    counts = jnp.concatenate([lower_half, upper_half], axis=1)
    perm_keys = jax.random.split(keys[4], N_ROW * N_COL)
    orders = jax.vmap(lambda single: jax.random.permutation(single, capacity))(perm_keys)
    orders = orders.reshape(N_ROW, N_COL, capacity)
    listed = (orders < counts[:, :, None]).astype(jnp.int32)
    listed = listed.reshape(N_ROW, N_COL, TR, TC).transpose(0, 2, 1, 3).reshape(NTR, NTC)
    column = jnp.broadcast_to(col_rank[None, :], (NTR, NTC))
    high_floor = jnp.maximum(S - column + 1, R // 8)
    high_rank = jax.random.randint(keys[5], (NTR, NTC), high_floor, R + 1)
    low_rank = jax.random.randint(keys[6], (NTR, NTC), R // 8, S - column + 1)
    tile_rank = jnp.where(listed == 1, high_rank, low_rank).astype(jnp.int32)
    return (col_rank.astype(jnp.int32), listed, tile_rank)


def draw_tile_rank(key, part):
    return joint_ranks(key)[2]


def draw_listed(key, part):
    return joint_ranks(key)[1]


def draw_col_rank(key, part):
    return joint_ranks(key)[0]


def with_ends(result, own_key, low, top_value):
    longest = result.shape.index(max(result.shape))
    spots = []
    for shift in (0, 1):
        where = [jax.random.randint(jax.random.fold_in(own_key, axis), (), 0, length) for axis, length in enumerate(result.shape)]
        where[longest] = (where[longest] + shift) % result.shape[longest]
        spots.append(tuple(where))
    return result.at[spots[0]].set(low).at[spots[1]].set(top_value)


def shard_levels(own_key, dims, cuts, low, high):
    level = 1.0
    for position, parts in cuts:
        steps = jax.random.uniform(jax.random.fold_in(jax.random.fold_in(own_key, 6), position), (parts,), jnp.float32, low / len(cuts), high / len(cuts))
        level = level * jnp.repeat(jnp.exp(steps), dims[position] // parts).reshape((-1,) + (1,) * (len(dims) - 1 - position))
    return level


def centred(stream_key, dims, deviation, bound, pieces=(), held_as=jnp.bfloat16):
    gain = shard_levels(stream_key, dims, pieces, -0.22, 0.18) if pieces else 1.0
    entries = jax.random.normal(stream_key, dims, jnp.float32) * deviation * gain
    return jnp.minimum(jnp.maximum(entries, -bound), bound).astype(held_as)


def setup_inputs(seed: int = 0) -> dict:
    seeds = jax.random.split(jax.random.key(seed), 12)
    tile_u = centred(seeds[0], (NTR, NTC, B, R), 1.0, 6.0, ((0, 4), (1, 8)))
    tile_v = centred(seeds[1], (NTR, NTC, B, R), R ** -0.5, 0.5, ((0, 4), (1, 8)))
    tile_rank = draw_tile_rank(jax.random.fold_in(seeds[11], 71), 0)
    listed = draw_listed(jax.random.fold_in(seeds[11], 71), 0)
    row_u = centred(seeds[4], (NTR, B, R), 1.0, 6.0, ((0, 4), (1, 8)))
    row_v = centred(seeds[5], (NTR, B, R), R ** -0.5, 0.5, ((0, 4), (1, 8)))
    row_rank = with_ends(jax.random.randint(seeds[6], (NTR,), R // 8, R + 1), jax.random.fold_in(seeds[6], 1), R // 8, R).astype(jnp.int32)
    col_u = centred(seeds[7], (NTC, B, R), 1.0, 6.0, ((0, 8), (1, 4)))
    col_v = centred(seeds[8], (NTC, B, R), R ** -0.5, 0.5, ((0, 8), (1, 4)))
    col_rank = draw_col_rank(jax.random.fold_in(seeds[11], 71), 0)
    sketch = centred(seeds[10], (B, S), B ** -0.5, 0.125)
    return {"tile_u": tile_u, "tile_v": tile_v, "tile_rank": tile_rank, "listed": listed, "row_u": row_u, "row_v": row_v, "row_rank": row_rank, "col_u": col_u, "col_v": col_v, "col_rank": col_rank, "sketch": sketch}


def masked(factor, rank):
    width = factor.shape[-1]
    keep = lax.broadcasted_iota(jnp.int32, (width,), 0) < rank[..., None]
    return factor * keep[..., None, :].astype(factor.dtype)

def shifted(block, rank):
    width = block.shape[-1]
    target = lax.broadcasted_iota(jnp.int32, (width, width), 1)
    source = lax.broadcasted_iota(jnp.int32, (width, width), 0)
    shift = (target[None] == source[None] + rank[:, None, None]).astype(jnp.float32)
    return jnp.einsum('jbr,jrc->jbc', block.astype(jnp.float32), shift)

def update_row(tile_u, tile_v, ranks, flags, pan_u, pan_v, col_u, col_v, sketch):
    f32 = jnp.float32
    core = jnp.einsum('br,jbs->jrs', pan_v.astype(f32), col_v.astype(f32)).astype(jnp.bfloat16)
    left = jnp.einsum('br,jrs->jbs', pan_u.astype(f32), core.astype(f32)).astype(jnp.bfloat16)
    plain_u = (tile_u.astype(f32) + shifted(left, ranks)).astype(jnp.bfloat16)
    plain_v = (tile_v.astype(f32) - shifted(col_u, ranks)).astype(jnp.bfloat16)
    unew = jnp.concatenate([tile_u, left], axis=-1)
    vnew = jnp.concatenate([tile_v, -col_u], axis=-1)
    proj = jnp.einsum('jbq,bs->jqs', vnew.astype(f32), sketch.astype(f32)).astype(jnp.bfloat16)
    span = jnp.einsum('jbq,jqs->jbs', unew.astype(f32), proj.astype(f32))
    gram = jnp.einsum('jbs,jbt->jst', span, span, precision=lax.Precision.HIGHEST)
    width = gram.shape[-1]
    level = jnp.trace(gram, axis1=1, axis2=2) / width
    eye = jnp.eye(width, dtype=jnp.float32)
    gram = gram + (0.01 * level + 1e-06)[:, None, None] * eye
    factor = jnp.linalg.cholesky(gram)
    basis = lax.linalg.triangular_solve(factor, span, left_side=False, lower=True, transpose_a=True)
    order = span.shape[1]
    new_u = (basis * jnp.sqrt(jnp.float32(order))).astype(jnp.bfloat16)
    coef = (jnp.einsum('jbq,jbs->jqs', unew.astype(f32), new_u.astype(f32)) / order).astype(jnp.bfloat16)
    new_v = jnp.einsum('jbq,jqs->jbs', vnew.astype(f32), coef.astype(f32)).astype(jnp.bfloat16)
    pick = flags[:, None, None] == 1
    return (jnp.where(pick, new_u, plain_u), jnp.where(pick, new_v, plain_v))

def reference(tile_u, tile_v, tile_rank, listed, row_u, row_v, row_rank, col_u, col_v, col_rank, sketch):
    tile_u = masked(tile_u, tile_rank)
    tile_v = masked(tile_v, tile_rank)
    row_u = masked(row_u, row_rank)
    row_v = masked(row_v, row_rank)
    col_u = masked(col_u, col_rank)
    col_v = masked(col_v, col_rank)

    def one_row(items):
        return update_row(items[0], items[1], items[2], items[3], items[4], items[5], col_u, col_v, sketch)
    return lax.map(one_row, (tile_u, tile_v, tile_rank, listed, row_u, row_v))
```

```python
import functools

import jax
import jax.numpy as jnp
from jax import lax
from jax.experimental import pallas as pl
from jax.experimental.pallas import tpu as pltpu
from jax.sharding import PartitionSpec as P

F32 = jnp.float32
BF16 = jnp.bfloat16
ANY = pl.BlockSpec(memory_space=pl.ANY)
SMEM = pl.BlockSpec(memory_space=pltpu.SMEM)
VMEM = pl.BlockSpec(memory_space=pltpu.VMEM)
MIB = 2**20


def dot(a, b, ca=1, cb=0):
    return lax.dot_general(a, b, (((ca,), (cb,)), ((), ())), preferred_element_type=F32)


def halves(x):
    high = x.astype(BF16)
    return high, (x - high.astype(F32)).astype(BF16)


def lanes(shape):
    return lax.broadcasted_iota(jnp.int32, shape, len(shape) - 1)


def rows_of(shape):
    return lax.broadcasted_iota(jnp.int32, shape, len(shape) - 2)


def local_kernel(rank_ref, u_ref, v_ref, st_ref, proj_ref, uu_ref):
    t = pl.program_id(0)
    proj = dot(st_ref[...], v_ref[0])
    keep = lanes(proj.shape) < rank_ref[t]
    proj_ref[0] = jnp.where(keep, proj, 0.0).astype(BF16)
    u = u_ref[0]
    uu_ref[0] = dot(u, u, 0, 0)


def core_kernel(masks, pos_ref, *refs):
    q_refs = refs[: len(masks)]
    mine_ref, other_ref, own_out, other_out = refs[len(masks) :]
    count, chunk, width = q_refs[0].shape
    depth = mine_ref.shape[2]
    sides = []
    for mask in masks:
        start = jnp.bitwise_xor(pos_ref[1], mask) * chunk
        piece = jnp.bitwise_xor(start // depth, pos_ref[0])
        inner = pl.multiple_of(start % depth, chunk)
        both = [ref[piece, 1, pl.ds(inner, chunk), :] for ref in (mine_ref, other_ref)]
        sides.append(jnp.concatenate(both, axis=1).astype(F32).T.astype(BF16))
    for t in range(0, count, 2):
        total = None
        for q_ref, side in zip(q_refs, sides):
            pair = jnp.concatenate([q_ref[t], q_ref[t + 1]], axis=1)
            part = dot(side, pair)
            total = part if total is None else total + part
        for k in range(2):
            block = total[:, k * width : (k + 1) * width]
            own_out[t + k] = block[:width]
            other_out[t + k] = block[width:]


def left_kernel(
    masks, pos_ref, row_rank_ref, col_rank_ref, own_ref, other_ref, u_ref, x_ref, st_ref, *refs
):
    p_refs = refs[: 2 * len(masks)]
    left_ref, gram_ref, core_ref, proj_ref = refs[2 * len(masks) :]
    t = pl.program_id(0)
    chunk = p_refs[0].shape[1]
    core = own_ref[0] + other_ref[0]
    keep = (lanes(core.shape) < row_rank_ref[t]) & (rows_of(core.shape) < col_rank_ref[0])
    core = jnp.where(keep, core, 0.0).astype(BF16)
    core_ref[0] = core
    total = None
    for k, mask in enumerate(masks):
        start = jnp.bitwise_xor(pos_ref[1] // 2, mask // 2) * (2 * chunk)
        start = pl.multiple_of(start, 2 * chunk)
        odd = pos_ref[1] % 2 == 1
        first, second = p_refs[2 * k][0], p_refs[2 * k + 1][0]
        panel = jnp.concatenate(
            [jnp.where(odd, second, first), jnp.where(odd, first, second)], axis=0
        )
        left = dot(panel, core, 1, 1).astype(BF16)
        left_ref[0, pl.ds(start, 2 * chunk), :] = left
        both = jnp.concatenate([u_ref[0, pl.ds(start, 2 * chunk), :], left], axis=1)
        part = dot(left, both, 0, 0)
        total = part if total is None else total + part
    gram_ref[0] = total

    @pl.when(t == 0)
    def _():
        pieces, depth = x_ref.shape[0], x_ref.shape[2]
        proj = None
        for k in range(pieces):
            start = jnp.bitwise_xor(pos_ref[0], k) * depth
            start = pl.multiple_of(start, depth)
            part = dot(st_ref[:, pl.ds(start, depth)], x_ref[k, 0])
            proj = part if proj is None else proj + part
        keep = lanes(proj.shape) < col_rank_ref[0]
        proj_ref[...] = jnp.where(keep, -proj, 0.0).astype(BF16)


def final_kernel(
    pos_ref,
    rank_ref,
    listed_ref,
    col_rank_ref,
    first_ref,
    second_ref,
    u_hbm,
    v_hbm,
    left_hbm,
    x_hbm,
    uu_ref,
    gram_ref,
    core_ref,
    vproj_ref,
    xproj_ref,
    out_u,
    out_v,
    u_buf,
    v_buf,
    left_buf,
    x_buf,
    to_u,
    to_v,
    gs,
    rs,
    ts,
    scales,
    sem_in,
    sem_x,
    sem_out,
    *,
    last_mask,
    block,
):
    count, order, width = u_hbm.shape
    chunk = first_ref.shape[1]
    pieces, depth = x_hbm.shape[0], x_hbm.shape[2]

    def fetch(which, t):
        src = (u_hbm, left_hbm, v_hbm)[which]
        dst = (u_buf, left_buf, v_buf)[which]
        return pltpu.make_async_copy(src.at[t], dst.at[t], sem_in.at[which, t])

    def fetch_x(k):
        start = jnp.bitwise_xor(pos_ref[0], k) * depth
        start = pl.multiple_of(start, depth)
        return pltpu.make_async_copy(x_hbm.at[k, 0], x_buf.at[pl.ds(start, depth), :], sem_x.at[k])

    def send(which, t):
        src = (to_u, to_v)[which]
        dst = (out_u, out_v)[which]
        return pltpu.make_async_copy(src.at[t], dst.at[t], sem_out.at[which, t])

    for t in range(count):
        fetch(0, t).start()
        fetch(1, t).start()
    for t in range(count):
        fetch(2, t).start()
    for k in range(pieces):
        fetch_x(k).start()

    odd = pos_ref[1] % 2 == 1
    start = jnp.bitwise_xor(pos_ref[1] // 2, last_mask // 2) * (2 * chunk)
    start = pl.multiple_of(start, 2 * chunk)
    square = (width, width)
    eye = rows_of(square) == lanes(square)

    def assemble(t, carry):
        fetch(0, t).wait()
        fetch(1, t).wait()
        first, second = first_ref[t], second_ref[t]
        panel = jnp.concatenate(
            [jnp.where(odd, second, first), jnp.where(odd, first, second)], axis=0
        )
        left = dot(panel, core_ref[t], 1, 1).astype(BF16)
        left_buf[t, pl.ds(start, 2 * chunk), :] = left
        both = jnp.concatenate([u_buf[t, pl.ds(start, 2 * chunk), :], left], axis=1)
        low = gram_ref[t] + dot(left, both, 0, 0)
        lu_h, lu_l = halves(low[:, :width])
        ll_h, ll_l = halves(low[:, width:])
        uu_h, uu_l = halves(uu_ref[t])
        a, b = vproj_ref[t], xproj_ref[...]
        left_part = dot(a, uu_h) + dot(a, uu_l) + dot(b, lu_h) + dot(b, lu_l)
        right_part = dot(a, lu_h, 1, 1) + dot(a, lu_l, 1, 1) + dot(b, ll_h) + dot(b, ll_l)
        moved = jnp.concatenate([left_part, right_part], axis=1)
        ts[t] = moved
        moved_h, moved_l = halves(moved)
        weights = jnp.concatenate([a, b], axis=1)
        gram = dot(moved_h, weights, 1, 1) + dot(moved_l, weights, 1, 1)
        diag = jnp.where(eye, gram, 0.0)
        trace = jnp.sum(jnp.sum(diag, axis=1, keepdims=True), axis=0, keepdims=True)
        scale = trace / width + 0.0001
        inverse = 1.0 / scale
        gs[pl.ds(pl.multiple_of(t * width, width), width), :] = gram * inverse + jnp.where(
            eye, 0.01, 0.0
        )
        scales[t] = jnp.broadcast_to(lax.rsqrt(scale), scales.shape[1:])
        return carry

    lax.fori_loop(0, count, assemble, 0)

    lane = lanes((count, width))
    for k0 in range(0, width, block):
        rows = [gs[pl.ds(k0 + r, count, stride=width), :] for r in range(block)]
        for k in range(block):
            at = k0 + k
            pivot = jnp.broadcast_to(rows[k][:, at : at + 1], (count, width))
            root = lax.rsqrt(pivot)
            inverse = root * root
            here = lane == at
            rs[pl.ds(at, count, stride=width), :] = jnp.where(here, 1.0, rows[k]) * root
            scaled = jnp.where(here, 1.0 + inverse, rows[k] * inverse)
            for r in range(k + 1, block):
                rows[r] = rows[r] - rows[r][:, at : at + 1] * scaled
        end = k0 + block
        if end < width:
            strip = (block, width)
            strip_lane = lanes(strip)
            own = k0 + rows_of(strip)
            for n in range(count):
                done = rs[pl.ds(n * width + k0, block), :]
                ahead = jnp.where(strip_lane >= end, done, 0.0)
                use = jnp.where((strip_lane > own) & (strip_lane < end), 0.0, done)
                a_h, a_l = halves(ahead)
                b_h, b_l = halves(use)
                a = jnp.concatenate([a_h, a_l, a_h], axis=0)
                b = jnp.concatenate([b_h, b_h, b_l], axis=0)
                change = dot(a, b, 0, 0)
                rest = pl.ds(n * width + end, width - end)
                old = gs[rest, :]
                gone = lanes(old.shape)
                old = jnp.where((gone >= k0) & (gone < end), 0.0, old)
                gs[rest, :] = old - change[end:]

    for k in range(pieces):
        fetch_x(k).wait()

    def finish(t, carry):
        tile_rank = rank_ref[t]
        picked = listed_ref[t] == 1
        inverse = rs[pl.ds(pl.multiple_of(t * width, width), width), :]
        inverse = jnp.where(lanes(square) <= rows_of(square), inverse, 0.0)
        inverse = inverse * (scales[t][:1, :1] * (float(order) ** 0.5))
        inv_h, inv_l = halves(inverse)
        weights = jnp.concatenate([vproj_ref[t], xproj_ref[...]], axis=1)
        mixed = dot(inv_h, weights) + dot(inv_l, weights)
        mixed_h, mixed_l = halves(mixed)
        moved_h, moved_l = halves(ts[t])
        coef = dot(inv_h, moved_h) + dot(inv_h, moved_l) + dot(inv_l, moved_h)
        coef = coef * (1.0 / order)
        wide = coef.shape
        col = lanes(wide)
        row = rows_of(wide)
        in_u = col < width
        keep = (col == row) & (col < tile_rank)
        moved_to = (col >= width) & (row == col - width + tile_rank)
        exact_u = jnp.where(keep | moved_to, 1.0, 0.0)
        moved_to = moved_to & (col - width < col_rank_ref[0])
        exact_v = jnp.where(keep, 1.0, jnp.where(moved_to, -1.0, 0.0))
        coef = jnp.where(in_u, jnp.where(col < tile_rank, coef, 0.0), -coef)
        coef = jnp.where(picked, coef, exact_v).astype(BF16)
        mixed_h = jnp.where(picked, mixed_h.astype(F32), exact_u).astype(BF16)
        mixed_l = jnp.where(picked, mixed_l.astype(F32), 0.0).astype(BF16)
        both = jnp.concatenate([mixed_h, mixed_l], axis=0)
        pair = jnp.concatenate([u_buf[t], left_buf[t]], axis=1)
        result = dot(pair, both, 1, 1)
        to_u[t] = (result[:, :width] + result[:, width:]).astype(BF16)
        send(0, t).start()
        fetch(2, t).wait()
        pair = jnp.concatenate([v_buf[t], x_buf[...]], axis=1)
        to_v[t] = dot(pair, coef, 1, 1).astype(BF16)
        send(1, t).start()
        return carry

    lax.fori_loop(0, count, finish, 0)

    def drain(t, carry):
        send(0, t).wait()
        send(1, t).wait()
        return carry

    lax.fori_loop(0, count, drain, 0)


def swap(x, axis, size, mask):
    return lax.ppermute(x, axis, [(c, c ^ mask) for c in range(size)])


def on_device(
    n_row,
    n_col,
    tile_u,
    tile_v,
    tile_rank,
    listed,
    row_u,
    row_v,
    row_rank,
    col_u,
    col_v,
    col_rank,
    sketch,
):
    rows_here, cols_here, order, width = tile_u.shape
    assert cols_here == 1 and width == sketch.shape[1]
    count = rows_here * cols_here
    chunk = row_u.shape[1]
    half = count // 2
    tile_u = tile_u.reshape(count, order, width)
    tile_v = tile_v.reshape(count, order, width)
    tile_rank = tile_rank.reshape(count)
    listed = listed.reshape(count)
    pos = jnp.stack([lax.axis_index("row"), lax.axis_index("col")]).astype(jnp.int32)
    col_swap = lambda x, mask: swap(x, "col", n_col, mask)
    dims = []
    mask = 2
    while mask < n_col:
        dims.append(mask)
        mask *= 2

    def spread(own, after=None):
        pieces = {0: own}
        first = [col_swap(own, m) for m in dims]
        for m, got in zip(dims, first):
            pieces[m] = got
        return pieces

    def spread_rest(pieces):
        if len(dims) == 2:
            low, high = dims
            a = col_swap(pieces[low][:half], high)
            b = col_swap(pieces[high][half:], low)
            pieces[low | high] = (a, b)
            return pieces
        for mask in range(2, n_col, 2):
            if mask not in pieces:
                bit = mask & -mask
                pieces[mask] = col_swap(pieces[mask ^ bit], bit)
        return pieces

    q = spread(row_v)
    sides = jnp.stack([col_u[0], col_v[0]])[None]
    mask = 1
    while mask < n_row:
        sides = jnp.concatenate([sides, swap(sides, "row", n_row, mask)], axis=0)
        mask *= 2
    sides_other = col_swap(sides, 1)
    turned = sketch.T

    vproj, uu = pl.pallas_call(
        local_kernel,
        grid_spec=pltpu.PrefetchScalarGridSpec(
            num_scalar_prefetch=1,
            grid=(count,),
            in_specs=[
                pl.BlockSpec((1, order, width), lambda t, r: (t, 0, 0)),
                pl.BlockSpec((1, order, width), lambda t, r: (t, 0, 0)),
                pl.BlockSpec((width, order), lambda t, r: (0, 0)),
            ],
            out_specs=[
                pl.BlockSpec((1, width, width), lambda t, r: (t, 0, 0)),
                pl.BlockSpec((1, width, width), lambda t, r: (t, 0, 0)),
            ],
        ),
        out_shape=[
            jax.ShapeDtypeStruct((count, width, width), BF16),
            jax.ShapeDtypeStruct((count, width, width), F32),
        ],
        compiler_params=pltpu.CompilerParams(vmem_limit_bytes=24 * MIB),
        cost_estimate=pl.CostEstimate(
            flops=4 * count * order * width * width,
            bytes_accessed=4 * count * order * width,
            transcendentals=0,
        ),
        name="local_products",
    )(tile_rank, tile_u, tile_v, turned)

    p_own, _ = lax.optimization_barrier((row_u, q[dims[-1]]))
    q = spread_rest(q)
    p = spread(p_own)
    masks = tuple(sorted(q))
    q_args = [
        jnp.concatenate(q[m], axis=0) if isinstance(q[m], tuple) else q[m] for m in masks
    ]
    part_shape = jax.ShapeDtypeStruct((count, width, width), F32)
    core_own, core_other = pl.pallas_call(
        functools.partial(core_kernel, masks),
        in_specs=[SMEM] + [VMEM] * (len(masks) + 2),
        out_specs=[VMEM, VMEM],
        out_shape=[part_shape, part_shape],
        compiler_params=pltpu.CompilerParams(vmem_limit_bytes=32 * MIB),
        cost_estimate=pl.CostEstimate(
            flops=2 * count * order * width * width,
            bytes_accessed=count * order * width,
            transcendentals=0,
        ),
        name="core_products",
    )(pos, *q_args, sides, sides_other)
    core_got = col_swap(core_other, 1)

    p = spread_rest(p)
    last = masks[-1]
    early = masks[:-1]
    mates = {m: col_swap(p[m], 1) for m in early}
    p_early = [x for m in early for x in (p[m], mates[m])]
    tile_spec = pl.BlockSpec((1, order, width), lambda t, *_: (t, 0, 0))
    small_spec = pl.BlockSpec((1, width, width), lambda t, *_: (t, 0, 0))
    piece_spec = pl.BlockSpec((1, chunk, width), lambda t, *_: (t, 0, 0))
    left, low, core, xproj = pl.pallas_call(
        functools.partial(left_kernel, early),
        grid_spec=pltpu.PrefetchScalarGridSpec(
            num_scalar_prefetch=3,
            grid=(count,),
            in_specs=[
                small_spec,
                small_spec,
                tile_spec,
                pl.BlockSpec(sides.shape, lambda t, *_: (0, 0, 0, 0)),
                pl.BlockSpec((width, order), lambda t, *_: (0, 0)),
            ]
            + [piece_spec] * len(p_early),
            out_specs=[
                tile_spec,
                pl.BlockSpec((1, width, 2 * width), lambda t, *_: (t, 0, 0)),
                small_spec,
                pl.BlockSpec((width, width), lambda t, *_: (0, 0)),
            ],
        ),
        out_shape=[
            jax.ShapeDtypeStruct((count, order, width), BF16),
            jax.ShapeDtypeStruct((count, width, 2 * width), F32),
            jax.ShapeDtypeStruct((count, width, width), BF16),
            jax.ShapeDtypeStruct((width, width), BF16),
        ],
        compiler_params=pltpu.CompilerParams(vmem_limit_bytes=32 * MIB),
        cost_estimate=pl.CostEstimate(
            flops=6 * count * order * width * width,
            bytes_accessed=6 * count * order * width,
            transcendentals=0,
        ),
        name="left_products",
    )(pos, row_rank, col_rank, core_own, core_got, tile_u, sides, turned, *p_early)

    tail = p[last]
    if isinstance(tail, tuple):
        mate = jnp.concatenate([col_swap(x, 1) for x in tail], axis=0)
        tail = jnp.concatenate(tail, axis=0)
    else:
        mate = col_swap(tail, 1)
    out_shape = jax.ShapeDtypeStruct((count, order, width), BF16)
    out_u, out_v = pl.pallas_call(
        functools.partial(final_kernel, last_mask=last, block=32),
        in_specs=[SMEM] * 4 + [VMEM] * 2 + [ANY] * 4 + [VMEM] * 5,
        out_specs=[ANY, ANY],
        out_shape=[out_shape, out_shape],
        scratch_shapes=[
            pltpu.VMEM((count, order, width), BF16),
            pltpu.VMEM((count, order, width), BF16),
            pltpu.VMEM((count, order, width), BF16),
            pltpu.VMEM((order, width), BF16),
            pltpu.VMEM((count, order, width), BF16),
            pltpu.VMEM((count, order, width), BF16),
            pltpu.VMEM((count * width, width), F32),
            pltpu.VMEM((count * width, width), F32),
            pltpu.VMEM((count, width, 2 * width), F32),
            pltpu.VMEM((count, 8, width), F32),
            pltpu.SemaphoreType.DMA((3, count)),
            pltpu.SemaphoreType.DMA((sides.shape[0],)),
            pltpu.SemaphoreType.DMA((2, count)),
        ],
        compiler_params=pltpu.CompilerParams(vmem_limit_bytes=48 * MIB),
        cost_estimate=pl.CostEstimate(
            flops=16 * count * order * width * width,
            bytes_accessed=10 * count * order * width,
            transcendentals=0,
        ),
        name="recompress_store",
    )(
        pos,
        tile_rank,
        listed,
        col_rank,
        tail,
        mate,
        tile_u,
        tile_v,
        left,
        sides,
        uu,
        low,
        core,
        vproj,
        xproj,
    )
    shape = (rows_here, cols_here, order, width)
    return out_u.reshape(shape), out_v.reshape(shape)


def solution(mesh):
    return jax.shard_map(
        functools.partial(on_device, mesh.shape["row"], mesh.shape["col"]),
        mesh=mesh,
        in_specs=(
            P("row", "col", None, None),
            P("row", "col", None, None),
            P("row", "col"),
            P("row", "col"),
            P("row", "col", None),
            P("row", "col", None),
            P("row"),
            P("col", "row", None),
            P("col", "row", None),
            P("col"),
            P(),
        ),
        out_specs=(P("row", "col", None, None), P("row", "col", None, None)),
        check_vma=False,
    )
```

```python
import functools

import jax
import jax.numpy as jnp
from jax import lax
from jax.experimental import pallas as pl
from jax.experimental.pallas import tpu as pltpu
from jax.sharding import PartitionSpec as P

F32 = jnp.float32
BF16 = jnp.bfloat16
HBM = pl.BlockSpec(memory_space=pltpu.HBM)
SMEM = pl.BlockSpec(memory_space=pltpu.SMEM)
VMEM = pl.BlockSpec(memory_space=pltpu.VMEM)
MIB = 2**20


def dot(a, b, ca=1, cb=0):
    return lax.dot_general(a, b, (((ca,), (cb,)), ((), ())), preferred_element_type=F32)


def halves(x):
    high = x.astype(BF16)
    return high, (x - high.astype(F32)).astype(BF16)


def lanes(shape):
    return lax.broadcasted_iota(jnp.int32, shape, len(shape) - 1)


def rows_of(shape):
    return lax.broadcasted_iota(jnp.int32, shape, len(shape) - 2)


def local_kernel(rank_ref, st_ref, u_ref, v_ref, proj_ref, uu_ref):
    for t in range(u_ref.shape[0]):
        proj = dot(st_ref[...], v_ref[t])
        keep = lanes(proj.shape) < rank_ref[t]
        proj_ref[t] = jnp.where(keep, proj, 0.0).astype(BF16)
        u = u_ref[t]
        uu_ref[t] = dot(u, u, 0, 0)


def core_kernel(pos_ref, *refs, masks, pieces, more):
    q_refs, refs = refs[: len(masks)], refs[len(masks) :]
    mine_refs, refs = refs[:pieces], refs[pieces:]
    other_ref, refs = refs[0], refs[1:]
    before, (own_out, other_out) = refs[:-2], refs[-2:]
    count, chunk, width = q_refs[0].shape
    depth = other_ref.shape[1]
    sides = []
    for mask in masks:
        start = jnp.bitwise_xor(pos_ref[1], mask) * chunk
        piece = lax.rem(pos_ref[0] + pieces - start // depth, pieces)
        inner = pl.multiple_of(start % depth, chunk)
        mine = mine_refs[0][0, pl.ds(inner, chunk), :]
        for k in range(1, pieces):
            mine = jnp.where(piece == k, mine_refs[k][0, pl.ds(inner, chunk), :], mine)
        both = [mine, other_ref[piece, pl.ds(inner, chunk), :]]
        sides.append(jnp.concatenate(both, axis=1).astype(F32).T.astype(BF16))
    for t in range(0, count, 2):
        total = None
        for q_ref, side in zip(q_refs, sides):
            pair = jnp.concatenate([q_ref[t], q_ref[t + 1]], axis=1)
            part = dot(side, pair)
            total = part if total is None else total + part
        for k in range(2):
            block = total[:, k * width : (k + 1) * width]
            own, other = block[:width], block[width:]
            if more:
                own, other = own + before[0][t + k], other + before[1][t + k]
            own_out[t + k] = own
            other_out[t + k] = other


def final_kernel(
    pos_ref,
    rank_ref,
    listed_ref,
    row_rank_ref,
    col_rank_ref,
    u_hbm,
    v_hbm,
    uu_ref,
    own_ref,
    other_ref,
    vproj_ref,
    st_ref,
    *refs,
    masks,
    block,
    pieces,
):
    x_refs, refs = refs[:pieces], refs[pieces:]
    panel_refs, refs = refs[: 2 * len(masks)], refs[2 * len(masks) :]
    (
        out_u,
        out_v,
        u_buf,
        v_buf,
        left_buf,
        x_buf,
        to_u,
        to_v,
        gs,
        rs,
        ts,
        scales,
        to_mix,
        to_coef,
        sem_u,
        sem_v,
        sem_out,
    ) = refs
    count, order, width = u_hbm.shape
    chunk = panel_refs[0].shape[1]
    depth = x_refs[0].shape[1]
    def rows_at(k):
        start = jnp.bitwise_xor(pos_ref[1], masks[k // 2] + k % 2) * chunk
        return pl.ds(pl.multiple_of(start, chunk), chunk)

    spans = [pl.ds(k * chunk, chunk) for k in range(len(panel_refs))]
    loads = [
        pltpu.make_async_copy(u_hbm.at[:, rows_at(k), :], u_buf.at[:, span, :], sem_u.at[k])
        for k, span in enumerate(spans)
    ]
    for copy in loads:
        copy.start()
    load_v = pltpu.make_async_copy(v_hbm, v_buf, sem_v)
    load_v.start()
    for k in range(pieces):
        start = lax.rem(pos_ref[0] + pieces - k, pieces) * depth
        rows = pl.ds(pl.multiple_of(start, depth), depth)
        x_buf[rows, :] = x_refs[k][0]

    def send_u(t, k):
        src = to_u.at[t, spans[k], :]
        return pltpu.make_async_copy(src, out_u.at[t, rows_at(k), :], sem_out.at[0])

    def send_v(t):
        return pltpu.make_async_copy(to_v.at[t], out_v.at[t], sem_out.at[1])

    square = (width, width)
    eye = rows_of(square) == lanes(square)
    xproj = dot(st_ref[...], x_buf[...])
    xproj = jnp.where(lanes(square) < col_rank_ref[0], -xproj, 0.0).astype(BF16)

    for t in range(count):
        core = own_ref[t] + other_ref[t]
        keep = (lanes(square) < row_rank_ref[t]) & (rows_of(square) < col_rank_ref[0])
        core = jnp.where(keep, core, 0.0).astype(BF16)
        panel = jnp.concatenate([ref[t] for ref in panel_refs], axis=0)
        left_buf[t] = dot(panel, core, 1, 1).astype(BF16)
    for copy in loads:
        copy.wait()

    def assemble(t):
        left = left_buf[t]
        low = dot(left, jnp.concatenate([u_buf[t], left], axis=1), 0, 0)
        lu_h, lu_l = halves(low[:, :width])
        ll_h, ll_l = halves(low[:, width:])
        uu_h, uu_l = halves(uu_ref[t])
        a, b = vproj_ref[t], xproj
        left_part = dot(a, uu_h) + dot(a, uu_l) + dot(b, lu_h) + dot(b, lu_l)
        right_part = dot(a, lu_h, 1, 1) + dot(a, lu_l, 1, 1) + dot(b, ll_h) + dot(b, ll_l)
        moved = jnp.concatenate([left_part, right_part], axis=1)
        ts[t] = moved
        moved_h, moved_l = halves(moved)
        weights = jnp.concatenate([a, b], axis=1)
        gram = dot(moved_h, weights, 1, 1) + dot(moved_l, weights, 1, 1)
        diag = jnp.where(eye, gram, 0.0)
        trace = jnp.sum(jnp.sum(diag, axis=1, keepdims=True), axis=0, keepdims=True)
        scale = trace / width + 0.0001
        inverse = 1.0 / scale
        gs[pl.ds(t * width, width), :] = gram * inverse + jnp.where(
            eye, 0.01, 0.0
        )
        scales[t] = jnp.broadcast_to(lax.rsqrt(scale), scales.shape[1:])

    for t in range(count):
        assemble(t)

    lane = lanes((count, width))
    small = 8
    for k0 in range(0, width, block):
        end = k0 + block
        taken = jnp.stack([gs[pl.ds(n * width + k0, block), :] for n in range(count)])
        taken = jnp.swapaxes(taken, 0, 1)
        rows = [taken[r] for r in range(block)]
        ready = []
        for b0 in range(0, block, small):
            first = k0 + b0
            inside = (lane >= first) & (lane < first + small)
            part = rows[b0 : b0 + small]
            a = [
                [part[i][:, first + j : first + j + 1] for j in range(i + 1)]
                for i in range(small)
            ]
            a = [[jnp.broadcast_to(x, (count, width)) for x in line] for line in a]
            part = [
                jnp.where(inside, jnp.where(lane == first + i, 1.0, 0.0), x)
                for i, x in enumerate(part)
            ]
            for j in range(small):
                root = lax.rsqrt(a[j][j])
                part[j] = part[j] * root
                factors = {i: a[i][j] * root for i in range(j + 1, small)}
                for i in range(j + 1, small):
                    for m in range(j + 1, i + 1):
                        a[i][m] = a[i][m] - factors[i] * factors[m]
                    part[i] = part[i] - factors[i] * part[j]
            for r in range(b0 + small, block):
                row = jnp.where(inside, 0.0, rows[r])
                for j in range(small):
                    row = row - part[j][:, k0 + r : k0 + r + 1] * part[j]
                rows[r] = row
            ready += part
        ready = jnp.swapaxes(jnp.stack(ready), 0, 1)
        for n in range(count):
            rs[pl.ds(n * width + k0, block), :] = ready[n]
        if end < width:
            strip = (block, width)
            strip_lane = lanes(strip)
            own = k0 + rows_of(strip)
            group = min(count, width // block)
            for g in range(0, count, group):
                ahead, use = [], []
                for n in range(g, g + group):
                    done = ready[n]
                    ahead.append(jnp.where(strip_lane >= end, done, 0.0))
                    use.append(
                        jnp.where((strip_lane > own) & (strip_lane < end), 0.0, done)
                    )
                turned = jnp.concatenate(ahead, axis=0).T[end:]
                a_h, a_l = halves(turned)
                both = jnp.concatenate([a_h, a_l], axis=1)
                for n in range(0, group, 2):
                    cells = []
                    for m in (n, n + 1):
                        spread = [jnp.zeros(strip, F32)] * group
                        spread[m] = use[m]
                        cells.append(jnp.concatenate(spread, axis=0))
                    b_h, b_l = halves(jnp.concatenate(cells, axis=1))
                    change = dot(both, jnp.concatenate([b_h, b_h], axis=0)) + dot(a_h, b_l)
                    for m in (n, n + 1):
                        rest = pl.ds((g + m) * width + end, width - end)
                        old = gs[rest, :]
                        gone = lanes(old.shape)
                        old = jnp.where((gone >= k0) & (gone < end), 0.0, old)
                        gs[rest, :] = old - change[:, (m - n) * width : (m - n + 1) * width]

    def weigh(t):
        tile_rank = rank_ref[t]
        picked = listed_ref[t] == 1
        inverse = rs[pl.ds(t * width, width), :]
        inverse = jnp.where(lanes(square) <= rows_of(square), inverse, 0.0)
        inverse = inverse * (scales[t][:1, :1] * (float(order) ** 0.5))
        inv_h, inv_l = halves(inverse)
        weights = jnp.concatenate([vproj_ref[t], xproj], axis=1)
        mixed = dot(inv_h, weights) + dot(inv_l, weights)
        mixed_h, mixed_l = halves(mixed)
        moved_h, moved_l = halves(ts[t])
        coef = dot(inv_h, moved_h) + dot(inv_h, moved_l) + dot(inv_l, moved_h)
        coef = coef * (1.0 / order)
        wide = coef.shape
        col = lanes(wide)
        row = rows_of(wide)
        in_u = col < width
        keep = (col == row) & (col < tile_rank)
        moved_to = (col >= width) & (row == col - width + tile_rank)
        exact_u = jnp.where(keep | moved_to, 1.0, 0.0)
        moved_to = moved_to & (col - width < col_rank_ref[0])
        exact_v = jnp.where(keep, 1.0, jnp.where(moved_to, -1.0, 0.0))
        coef = jnp.where(in_u, jnp.where(col < tile_rank, coef, 0.0), -coef)
        coef = jnp.where(picked, coef, exact_v).astype(BF16)
        mixed_h = jnp.where(picked, mixed_h.astype(F32), exact_u).astype(BF16)
        mixed_l = jnp.where(picked, mixed_l.astype(F32), 0.0).astype(BF16)
        both = jnp.concatenate([mixed_h, mixed_l], axis=0)
        to_mix[t] = both
        to_coef[t] = coef

    for t in range(count):
        weigh(t)
    load_v.wait()

    def finish(t, carry):
        side = jnp.concatenate([u_buf[t], left_buf[t]], axis=1)
        result = dot(side, to_mix[t], 1, 1)
        to_u[t] = (result[:, :width] + result[:, width:]).astype(BF16)
        for k in range(len(spans)):
            send_u(t, k).start()
        side = jnp.concatenate([v_buf[t], x_buf[...]], axis=1)
        to_v[t] = dot(side, to_coef[t], 1, 1).astype(BF16)
        send_v(t).start()
        return carry

    lax.fori_loop(0, count, finish, 0)
    pltpu.make_async_copy(to_u, out_u, sem_out.at[0]).wait()
    pltpu.make_async_copy(to_v, out_v, sem_out.at[1]).wait()


def swap(x, axis, size, mask):
    return lax.ppermute(x, axis, [(c, c ^ mask) for c in range(size)])


def on_device(
    n_row,
    n_col,
    tile_u,
    tile_v,
    tile_rank,
    listed,
    row_u,
    row_v,
    row_rank,
    col_u,
    col_v,
    col_rank,
    sketch,
):
    rows_here, cols_here, order, width = tile_u.shape
    assert cols_here == 1 and width == sketch.shape[1]
    count = rows_here * cols_here
    chunk = row_u.shape[1]
    tile_u = tile_u.reshape(count, order, width)
    tile_v = tile_v.reshape(count, order, width)
    tile_rank = tile_rank.reshape(count)
    listed = listed.reshape(count)
    pos = jnp.stack([lax.axis_index("row"), lax.axis_index("col")]).astype(jnp.int32)
    col_swap = lambda x, mask: swap(x, "col", n_col, mask)
    dims = []
    mask = 2
    while mask < n_col:
        dims.append(mask)
        mask *= 2

    tie = lax.optimization_barrier

    def gather(own, order, found):
        for m in order:
            for r in sorted(found):
                if not r & m and r | m not in found:
                    found[r | m] = col_swap(found[r], m)
        return found

    ring = [(c, (c + 1) % n_row) for c in range(n_row)]
    q = {0: row_v, **{m: col_swap(row_v, m) for m in dims}}
    p = {0: row_u, **{m: col_swap(row_u, m) for m in dims}}
    y = [col_v]
    for _ in range(n_row - 2):
        y.append(lax.ppermute(y[-1], "row", ring))
    turned = sketch.T

    vproj, uu = pl.pallas_call(
        local_kernel,
        in_specs=[SMEM, VMEM, VMEM, VMEM],
        out_specs=[VMEM, VMEM],
        out_shape=[
            jax.ShapeDtypeStruct((count, width, width), BF16),
            jax.ShapeDtypeStruct((count, width, width), F32),
        ],
        compiler_params=pltpu.CompilerParams(vmem_limit_bytes=16 * MIB),
        cost_estimate=pl.CostEstimate(
            flops=4 * count * order * width * width,
            bytes_accessed=4 * count * order * width,
            transcendentals=0,
        ),
        name="local_products",
    )(tile_rank, turned, tile_u, tile_v)

    passed, vproj, x_own, q[dims[0]], p[dims[-1]] = tie(
        (y[-1], vproj, col_u, q[dims[0]], p[dims[-1]])
    )
    y.append(lax.ppermute(passed, "row", ring))
    x = [x_own, lax.ppermute(x_own, "row", ring)]
    q, p, vproj, uu, x = tie((q, p, vproj, uu, x))
    for _ in range(n_row - 2):
        x.append(lax.ppermute(x[-1], "row", ring))
    q = gather(row_v, dims, q)
    p = gather(row_u, dims[::-1], p)
    y_other = col_swap(jnp.concatenate(y, axis=0), 1)
    own_mate = col_swap(row_u, 1)
    masks = tuple(range(0, n_col, 2))
    part_shape = jax.ShapeDtypeStruct((count, width, width), F32)

    def cores(use, before):
        return pl.pallas_call(
            functools.partial(core_kernel, masks=use, pieces=n_row, more=len(before) > 0),
            in_specs=[SMEM] + [VMEM] * (len(use) + n_row + 1 + len(before)),
            out_specs=[VMEM, VMEM],
            out_shape=[part_shape, part_shape],
            compiler_params=pltpu.CompilerParams(vmem_limit_bytes=16 * MIB),
            cost_estimate=pl.CostEstimate(
                flops=4 * len(use) * count * chunk * width * width,
                bytes_accessed=2 * len(use) * count * chunk * width,
                transcendentals=0,
            ),
            name="core_products",
        )(pos, *[q[m] for m in use], *y, y_other, *before)

    parts = cores(masks[:-1], []) if len(masks) > 1 else []
    parts, x = tie((parts, x))
    core_own, core_other = cores(masks[-1:], parts)
    core_got = col_swap(core_other, 1)

    panels = [row_u, own_mate]
    for m in masks[1:]:
        panels += [p[m], col_swap(p[m], 1)]
    out_shape = jax.ShapeDtypeStruct((count, order, width), BF16)
    out_u, out_v = pl.pallas_call(
        functools.partial(
            final_kernel,
            masks=masks,
            block=32,
            pieces=n_row,
        ),
        in_specs=[SMEM] * 5 + [HBM] * 2 + [VMEM] * (5 + n_row + len(panels)),
        out_specs=[HBM, HBM],
        out_shape=[out_shape, out_shape],
        scratch_shapes=[
            pltpu.VMEM((count, order, width), BF16),
            pltpu.VMEM((count, order, width), BF16),
            pltpu.VMEM((count, order, width), BF16),
            pltpu.VMEM((order, width), BF16),
            pltpu.VMEM((count, order, width), BF16),
            pltpu.VMEM((count, order, width), BF16),
            pltpu.VMEM((count * width, width), F32),
            pltpu.VMEM((count * width, width), F32),
            pltpu.VMEM((count, width, 2 * width), F32),
            pltpu.VMEM((count, 8, width), F32),
            pltpu.VMEM((count, 2 * width, 2 * width), BF16),
            pltpu.VMEM((count, width, 2 * width), BF16),
            pltpu.SemaphoreType.DMA((len(panels),)),
            pltpu.SemaphoreType.DMA,
            pltpu.SemaphoreType.DMA((2,)),
        ],
        compiler_params=pltpu.CompilerParams(vmem_limit_bytes=40 * MIB),
        cost_estimate=pl.CostEstimate(
            flops=16 * count * order * width * width,
            bytes_accessed=10 * count * order * width,
            transcendentals=0,
        ),
        name="recompress_store",
    )(
        pos,
        tile_rank,
        listed,
        row_rank,
        col_rank,
        tile_u,
        tile_v,
        uu,
        core_own,
        core_got,
        vproj,
        turned,
        *x,
        *panels,
    )
    shape = (rows_here, cols_here, order, width)
    return out_u.reshape(shape), out_v.reshape(shape)


def solution(mesh):
    return jax.shard_map(
        functools.partial(on_device, mesh.shape["row"], mesh.shape["col"]),
        mesh=mesh,
        in_specs=(
            P("row", "col", None, None),
            P("row", "col", None, None),
            P("row", "col"),
            P("row", "col"),
            P("row", "col", None),
            P("row", "col", None),
            P("row"),
            P("col", "row", None),
            P("col", "row", None),
            P("col"),
            P(),
        ),
        out_specs=(P("row", "col", None, None), P("row", "col", None, None)),
        check_vma=False,
    )
```

```python
import functools

import jax
import jax.numpy as jnp
from jax import lax
from jax.experimental import pallas as pl
from jax.experimental.pallas import tpu as pltpu
from jax.sharding import PartitionSpec as P

F32 = jnp.float32
BF16 = jnp.bfloat16
HBM = pl.BlockSpec(memory_space=pltpu.HBM)
SMEM = pl.BlockSpec(memory_space=pltpu.SMEM)
VMEM = pl.BlockSpec(memory_space=pltpu.VMEM)
MIB = 2**20


def dot(a, b, ca=1, cb=0):
    return lax.dot_general(a, b, (((ca,), (cb,)), ((), ())), preferred_element_type=F32)


def halves(x):
    high = x.astype(BF16)
    return high, (x - high.astype(F32)).astype(BF16)


def lanes(shape):
    return lax.broadcasted_iota(jnp.int32, shape, len(shape) - 1)


def rows_of(shape):
    return lax.broadcasted_iota(jnp.int32, shape, len(shape) - 2)


def gram_kernel(u_ref, uu_ref):
    for t in range(u_ref.shape[0]):
        u = u_ref[t]
        uu_ref[t] = dot(u, u, 0, 0)


def proj_kernel(rank_ref, st_ref, v_ref, proj_ref):
    for t in range(v_ref.shape[0]):
        proj = dot(st_ref[...], v_ref[t])
        keep = lanes(proj.shape) < rank_ref[t]
        proj_ref[t] = jnp.where(keep, proj, 0.0).astype(BF16)


def core_kernel(pos_ref, *refs, masks, pieces, more):
    q_refs, refs = refs[: len(masks)], refs[len(masks) :]
    mine_refs, refs = refs[:pieces], refs[pieces:]
    other_ref, refs = refs[0], refs[1:]
    before, (own_out, other_out) = refs[:-2], refs[-2:]
    count, chunk, width = q_refs[0].shape
    depth = other_ref.shape[1]
    sides = []
    for mask in masks:
        start = jnp.bitwise_xor(pos_ref[1], mask) * chunk
        piece = lax.rem(pos_ref[0] + pieces - start // depth, pieces)
        inner = pl.multiple_of(start % depth, chunk)
        mine = mine_refs[0][0, pl.ds(inner, chunk), :]
        for k in range(1, pieces):
            mine = jnp.where(piece == k, mine_refs[k][0, pl.ds(inner, chunk), :], mine)
        both = [mine, other_ref[piece, pl.ds(inner, chunk), :]]
        sides.append(jnp.concatenate(both, axis=1).astype(F32).T.astype(BF16))
    for t in range(0, count, 2):
        total = None
        for q_ref, side in zip(q_refs, sides):
            pair = jnp.concatenate([q_ref[t], q_ref[t + 1]], axis=1)
            part = dot(side, pair)
            total = part if total is None else total + part
        for k in range(2):
            block = total[:, k * width : (k + 1) * width]
            own, other = block[:width], block[width:]
            if more:
                own, other = own + before[0][t + k], other + before[1][t + k]
            own_out[t + k] = own
            other_out[t + k] = other


def final_kernel(
    pos_ref,
    rank_ref,
    listed_ref,
    row_rank_ref,
    col_rank_ref,
    u_hbm,
    v_hbm,
    uu_ref,
    own_ref,
    other_ref,
    vproj_ref,
    st_ref,
    *refs,
    masks,
    block,
    pieces,
):
    x_refs, refs = refs[:pieces], refs[pieces:]
    panel_refs, refs = refs[: 2 * len(masks)], refs[2 * len(masks) :]
    (
        out_u,
        out_v,
        u_buf,
        v_buf,
        left_buf,
        x_buf,
        to_u,
        to_v,
        gs,
        rs,
        ts,
        scales,
        mixes,
        to_mix,
        to_coef,
        sem_u,
        sem_v,
        sem_out,
    ) = refs
    count, order, width = u_hbm.shape
    chunk = panel_refs[0].shape[1]
    depth = x_refs[0].shape[1]
    def rows_at(k):
        start = jnp.bitwise_xor(pos_ref[1], masks[k // 2] + k % 2) * chunk
        return pl.ds(pl.multiple_of(start, chunk), chunk)

    spans = [pl.ds(k * chunk, chunk) for k in range(len(panel_refs))]
    loads = [
        pltpu.make_async_copy(u_hbm.at[:, rows_at(k), :], u_buf.at[:, span, :], sem_u.at[k])
        for k, span in enumerate(spans)
    ]
    for copy in loads:
        copy.start()
    load_v = pltpu.make_async_copy(v_hbm, v_buf, sem_v)
    load_v.start()
    for k in range(pieces):
        start = lax.rem(pos_ref[0] + pieces - k, pieces) * depth
        rows = pl.ds(pl.multiple_of(start, depth), depth)
        x_buf[rows, :] = x_refs[k][0]

    def send_u(t, k):
        src = to_u.at[t, spans[k], :]
        return pltpu.make_async_copy(src, out_u.at[t, rows_at(k), :], sem_out.at[0])

    def send_v(t):
        return pltpu.make_async_copy(to_v.at[t], out_v.at[t], sem_out.at[1])

    square = (width, width)
    eye = rows_of(square) == lanes(square)
    xproj = dot(st_ref[...], x_buf[...])
    xproj = jnp.where(lanes(square) < col_rank_ref[0], -xproj, 0.0).astype(BF16)

    for t in range(count):
        core = own_ref[t] + other_ref[t]
        keep = (lanes(square) < row_rank_ref[t]) & (rows_of(square) < col_rank_ref[0])
        core = jnp.where(keep, core, 0.0).astype(BF16)
        panel = jnp.concatenate([ref[t] for ref in panel_refs], axis=0)
        left_buf[t] = dot(panel, core, 1, 1).astype(BF16)
    for copy in loads:
        copy.wait()

    for t in range(count):
        left = left_buf[t]
        ts[t] = dot(left, jnp.concatenate([u_buf[t], left], axis=1), 0, 0)
    b = xproj
    for t in range(count):
        low = ts[t]
        lu_h, lu_l = halves(low[:, :width])
        ll_h, ll_l = halves(low[:, width:])
        uu_h, uu_l = halves(uu_ref[t])
        a = vproj_ref[t]
        left_part = dot(a, uu_h) + dot(a, uu_l) + dot(b, lu_h) + dot(b, lu_l)
        right_part = dot(a, lu_h, 1, 1) + dot(a, lu_l, 1, 1) + dot(b, ll_h) + dot(b, ll_l)
        ts[t] = jnp.concatenate([left_part, right_part], axis=1)
    for t in range(count):
        moved_h, moved_l = halves(ts[t])
        weights = jnp.concatenate([vproj_ref[t], b], axis=1)
        gs[pl.ds(t * width, width), :] = dot(moved_h, weights, 1, 1) + dot(moved_l, weights, 1, 1)
    for t in range(count):
        at = pl.ds(t * width, width)
        gram = gs[at, :]
        diag = jnp.where(eye, gram, 0.0)
        trace = jnp.sum(jnp.sum(diag, axis=1, keepdims=True), axis=0, keepdims=True)
        scale = trace / width + 0.0001
        gs[at, :] = gram * (1.0 / scale) + jnp.where(eye, 0.01, 0.0)
        scales[t] = jnp.broadcast_to(lax.rsqrt(scale), scales.shape[1:])

    lane = lanes((count, width))
    small = 8
    for k0 in range(0, width, block):
        end = k0 + block
        taken = jnp.stack([gs[pl.ds(n * width + k0, block), :] for n in range(count)])
        taken = jnp.swapaxes(taken, 0, 1)
        rows = [taken[r] for r in range(block)]
        ready = []
        for b0 in range(0, block, small):
            first = k0 + b0
            inside = (lane >= first) & (lane < first + small)
            part = rows[b0 : b0 + small]
            a = [
                [part[i][:, first + j : first + j + 1] for j in range(i + 1)]
                for i in range(small)
            ]
            a = [[jnp.broadcast_to(x, (count, width)) for x in line] for line in a]
            part = [
                jnp.where(inside, jnp.where(lane == first + i, 1.0, 0.0), x)
                for i, x in enumerate(part)
            ]
            for j in range(small):
                root = lax.rsqrt(a[j][j])
                part[j] = part[j] * root
                factors = {i: a[i][j] * root for i in range(j + 1, small)}
                for i in range(j + 1, small):
                    for m in range(j + 1, i + 1):
                        a[i][m] = a[i][m] - factors[i] * factors[m]
                    part[i] = part[i] - factors[i] * part[j]
            for r in range(b0 + small, block):
                row = jnp.where(inside, 0.0, rows[r])
                for j in range(small):
                    row = row - part[j][:, k0 + r : k0 + r + 1] * part[j]
                rows[r] = row
            ready += part
        ready = jnp.swapaxes(jnp.stack(ready), 0, 1)
        for n in range(count):
            rs[pl.ds(n * width + k0, block), :] = ready[n]
        if end < width:
            strip = (block, width)
            strip_lane = lanes(strip)
            own = k0 + rows_of(strip)
            group = min(count, width // block)
            ahead, use = [], []
            for n in range(count):
                done = ready[n]
                ahead.append(jnp.where(strip_lane >= end, done, 0.0))
                use.append(jnp.where((strip_lane > own) & (strip_lane < end), 0.0, done))
            changes = []
            for g in range(0, count, group):
                a_h, a_l = halves(jnp.concatenate(ahead[g : g + group], axis=0).T[end:])
                both = jnp.concatenate([a_h, a_l], axis=1)
                for n in range(0, group, 2):
                    cells = []
                    for m in (n, n + 1):
                        spread = [jnp.zeros(strip, F32)] * group
                        spread[m] = use[g + m]
                        cells.append(jnp.concatenate(spread, axis=0))
                    b_h, b_l = halves(jnp.concatenate(cells, axis=1))
                    change = dot(both, jnp.concatenate([b_h, b_h], axis=0)) + dot(a_h, b_l)
                    changes += [change[:, :width], change[:, width:]]
            for n in range(count):
                rest = pl.ds(n * width + end, width - end)
                old = gs[rest, :]
                gone = lanes(old.shape)
                gs[rest, :] = jnp.where((gone >= k0) & (gone < end), 0.0, old) - changes[n]

    for t in range(count):
        at = pl.ds(t * width, width)
        inverse = jnp.where(lanes(square) <= rows_of(square), rs[at, :], 0.0)
        rs[at, :] = inverse * (scales[t][:1, :1] * (float(order) ** 0.5))
    for t in range(count):
        inv_h, inv_l = halves(rs[pl.ds(t * width, width), :])
        weights = jnp.concatenate([vproj_ref[t], b], axis=1)
        mixes[t] = dot(inv_h, weights) + dot(inv_l, weights)
        moved_h, moved_l = halves(ts[t])
        ts[t] = dot(inv_h, moved_h) + dot(inv_h, moved_l) + dot(inv_l, moved_h)
    for t in range(count):
        tile_rank = rank_ref[t]
        picked = listed_ref[t] == 1
        mixed_h, mixed_l = halves(mixes[t])
        coef = ts[t]
        coef = coef * (1.0 / order)
        wide = coef.shape
        col = lanes(wide)
        row = rows_of(wide)
        in_u = col < width
        keep = (col == row) & (col < tile_rank)
        moved_to = (col >= width) & (row == col - width + tile_rank)
        exact_u = jnp.where(keep | moved_to, 1.0, 0.0)
        moved_to = moved_to & (col - width < col_rank_ref[0])
        exact_v = jnp.where(keep, 1.0, jnp.where(moved_to, -1.0, 0.0))
        coef = jnp.where(in_u, jnp.where(col < tile_rank, coef, 0.0), -coef)
        coef = jnp.where(picked, coef, exact_v).astype(BF16)
        mixed_h = jnp.where(picked, mixed_h.astype(F32), exact_u).astype(BF16)
        mixed_l = jnp.where(picked, mixed_l.astype(F32), 0.0).astype(BF16)
        both = jnp.concatenate([mixed_h, mixed_l], axis=0)
        to_mix[t] = both
        to_coef[t] = coef

    load_v.wait()

    def finish(t):
        side = jnp.concatenate([u_buf[t], left_buf[t]], axis=1)
        result = dot(side, to_mix[t], 1, 1)
        to_u[t] = (result[:, :width] + result[:, width:]).astype(BF16)
        for k in range(len(spans)):
            send_u(t, k).start()
        side = jnp.concatenate([v_buf[t], x_buf[...]], axis=1)
        to_v[t] = dot(side, to_coef[t], 1, 1).astype(BF16)
        send_v(t).start()

    for t in range(count):
        finish(t)
    pltpu.make_async_copy(to_u, out_u, sem_out.at[0]).wait()
    pltpu.make_async_copy(to_v, out_v, sem_out.at[1]).wait()


def swap(x, axis, size, mask):
    return lax.ppermute(x, axis, [(c, c ^ mask) for c in range(size)])


def on_device(
    n_row,
    n_col,
    tile_u,
    tile_v,
    tile_rank,
    listed,
    row_u,
    row_v,
    row_rank,
    col_u,
    col_v,
    col_rank,
    sketch,
):
    rows_here, cols_here, order, width = tile_u.shape
    assert cols_here == 1 and width == sketch.shape[1]
    count = rows_here * cols_here
    chunk = row_u.shape[1]
    tile_u = tile_u.reshape(count, order, width)
    tile_v = tile_v.reshape(count, order, width)
    tile_rank = tile_rank.reshape(count)
    listed = listed.reshape(count)
    pos = jnp.stack([lax.axis_index("row"), lax.axis_index("col")]).astype(jnp.int32)
    col_swap = lambda x, mask: swap(x, "col", n_col, mask)
    dims = []
    mask = 2
    while mask < n_col:
        dims.append(mask)
        mask *= 2

    tie = lax.optimization_barrier

    def gather(own, order, found):
        for m in order:
            for r in sorted(found):
                if not r & m and r | m not in found:
                    found[r | m] = col_swap(found[r], m)
        return found

    def shift(v, step):
        return lax.ppermute(v, "row", [(c, (c + step) % n_row) for c in range(n_row)])

    q = {0: row_v, **{m: col_swap(row_v, m) for m in dims}}
    p = {0: row_u, **{m: col_swap(row_u, m) for m in dims}}
    y = [col_v]
    for _ in range(n_row - 2):
        y.append(shift(y[-1], 1))
    cost = pl.CostEstimate(
        flops=2 * count * order * width * width,
        bytes_accessed=2 * count * order * width,
        transcendentals=0,
    )
    uu = pl.pallas_call(
        gram_kernel,
        in_specs=[VMEM],
        out_specs=VMEM,
        out_shape=jax.ShapeDtypeStruct((count, width, width), F32),
        compiler_params=pltpu.CompilerParams(vmem_limit_bytes=16 * MIB),
        cost_estimate=cost,
        name="gram_products",
    )(tile_u)
    y[-1], x_own, q[dims[0]], p[dims[-1]], uu = tie(
        (y[-1], col_u, q[dims[0]], p[dims[-1]], uu)
    )
    y.append(shift(y[-1], 1))
    x = [x_own, shift(x_own, 1)]
    q, p, x, tile_v, sketch = tie((q, p, x, tile_v, sketch))
    turned = sketch.T
    vproj = pl.pallas_call(
        proj_kernel,
        in_specs=[SMEM, VMEM, VMEM],
        out_specs=VMEM,
        out_shape=jax.ShapeDtypeStruct((count, width, width), BF16),
        compiler_params=pltpu.CompilerParams(vmem_limit_bytes=16 * MIB),
        cost_estimate=cost,
        name="sketch_products",
    )(tile_rank, turned, tile_v)
    back = shift(x[0], -1)
    for _ in range(n_row - 3):
        x.append(shift(x[-1], 1))
    x.append(back)
    q = gather(row_v, dims, q)
    p = gather(row_u, dims[::-1], p)
    y_other = col_swap(jnp.concatenate(y, axis=0), 1)
    own_mate = col_swap(row_u, 1)
    masks = tuple(range(0, n_col, 2))
    part_shape = jax.ShapeDtypeStruct((count, width, width), F32)

    def cores(use, before):
        return pl.pallas_call(
            functools.partial(core_kernel, masks=use, pieces=n_row, more=len(before) > 0),
            in_specs=[SMEM] + [VMEM] * (len(use) + n_row + 1 + len(before)),
            out_specs=[VMEM, VMEM],
            out_shape=[part_shape, part_shape],
            compiler_params=pltpu.CompilerParams(vmem_limit_bytes=16 * MIB),
            cost_estimate=pl.CostEstimate(
                flops=4 * len(use) * count * chunk * width * width,
                bytes_accessed=2 * len(use) * count * chunk * width,
                transcendentals=0,
            ),
            name="core_products",
        )(pos, *[q[m] for m in use], *y, y_other, *before)

    parts = cores(masks[:-1], []) if len(masks) > 1 else []
    parts, x, vproj = tie((parts, x, vproj))
    core_own, core_other = cores(masks[-1:], parts)
    core_got = col_swap(core_other, 1)

    panels = [row_u, own_mate]
    for m in masks[1:]:
        panels += [p[m], col_swap(p[m], 1)]
    out_shape = jax.ShapeDtypeStruct((count, order, width), BF16)
    out_u, out_v = pl.pallas_call(
        functools.partial(
            final_kernel,
            masks=masks,
            block=32,
            pieces=n_row,
        ),
        in_specs=[SMEM] * 5 + [HBM] * 2 + [VMEM] * (5 + n_row + len(panels)),
        out_specs=[HBM, HBM],
        out_shape=[out_shape, out_shape],
        scratch_shapes=[
            pltpu.VMEM((count, order, width), BF16),
            pltpu.VMEM((count, order, width), BF16),
            pltpu.VMEM((count, order, width), BF16),
            pltpu.VMEM((order, width), BF16),
            pltpu.VMEM((count, order, width), BF16),
            pltpu.VMEM((count, order, width), BF16),
            pltpu.VMEM((count * width, width), F32),
            pltpu.VMEM((count * width, width), F32),
            pltpu.VMEM((count, width, 2 * width), F32),
            pltpu.VMEM((count, 8, width), F32),
            pltpu.VMEM((count, width, 2 * width), F32),
            pltpu.VMEM((count, 2 * width, 2 * width), BF16),
            pltpu.VMEM((count, width, 2 * width), BF16),
            pltpu.SemaphoreType.DMA((len(panels),)),
            pltpu.SemaphoreType.DMA,
            pltpu.SemaphoreType.DMA((2,)),
        ],
        compiler_params=pltpu.CompilerParams(vmem_limit_bytes=40 * MIB),
        cost_estimate=pl.CostEstimate(
            flops=16 * count * order * width * width,
            bytes_accessed=10 * count * order * width,
            transcendentals=0,
        ),
        name="recompress_store",
    )(
        pos,
        tile_rank,
        listed,
        row_rank,
        col_rank,
        tile_u,
        tile_v,
        uu,
        core_own,
        core_got,
        vproj,
        turned,
        *x,
        *panels,
    )
    shape = (rows_here, cols_here, order, width)
    return out_u.reshape(shape), out_v.reshape(shape)


def solution(mesh):
    return jax.shard_map(
        functools.partial(on_device, mesh.shape["row"], mesh.shape["col"]),
        mesh=mesh,
        in_specs=(
            P("row", "col", None, None),
            P("row", "col", None, None),
            P("row", "col"),
            P("row", "col"),
            P("row", "col", None),
            P("row", "col", None),
            P("row"),
            P("col", "row", None),
            P("col", "row", None),
            P("col"),
            P(),
        ),
        out_specs=(P("row", "col", None, None), P("row", "col", None, None)),
        check_vma=False,
    )
```

```python
import functools

import jax
import jax.numpy as jnp
from jax import lax
from jax.experimental import pallas as pl
from jax.experimental.pallas import tpu as pltpu
from jax.sharding import PartitionSpec as P

F32 = jnp.float32
BF16 = jnp.bfloat16
HBM = pl.BlockSpec(memory_space=pltpu.HBM)
SMEM = pl.BlockSpec(memory_space=pltpu.SMEM)
VMEM = pl.BlockSpec(memory_space=pltpu.VMEM)
MIB = 2**20


def dot(a, b, ca=1, cb=0):
    return lax.dot_general(a, b, (((ca,), (cb,)), ((), ())), preferred_element_type=F32)


def halves(x):
    high = x.astype(BF16)
    return high, (x - high.astype(F32)).astype(BF16)


def lanes(shape):
    return lax.broadcasted_iota(jnp.int32, shape, len(shape) - 1)


def rows_of(shape):
    return lax.broadcasted_iota(jnp.int32, shape, len(shape) - 2)


def gram_kernel(u_ref, uu_ref):
    for t in range(u_ref.shape[0]):
        u = u_ref[t]
        uu_ref[t] = dot(u, u, 0, 0)


def proj_kernel(rank_ref, st_ref, v_ref, proj_ref):
    for t in range(v_ref.shape[0]):
        proj = dot(st_ref[...], v_ref[t])
        keep = lanes(proj.shape) < rank_ref[t]
        proj_ref[t] = jnp.where(keep, proj, 0.0).astype(BF16)


def core_kernel(pos_ref, *refs, masks, pieces, more, outs):
    q_refs, refs = refs[: len(masks)], refs[len(masks) :]
    mine_refs, refs = refs[:pieces], refs[pieces:]
    other_ref, refs = refs[0], refs[1:]
    before, out_refs = refs[: -len(outs)], refs[-len(outs) :]
    count, chunk, width = q_refs[0].shape
    depth = other_ref.shape[1]
    sides = []
    for mask in masks:
        start = jnp.bitwise_xor(pos_ref[1], mask) * chunk
        piece = lax.rem(pos_ref[0] + pieces - start // depth, pieces)
        inner = pl.multiple_of(start % depth, chunk)
        mine = mine_refs[0][0, pl.ds(inner, chunk), :]
        for k in range(1, pieces):
            mine = jnp.where(piece == k, mine_refs[k][0, pl.ds(inner, chunk), :], mine)
        both = [mine, other_ref[piece, pl.ds(inner, chunk), :]]
        both = [both[k] for k in outs]
        sides.append(jnp.concatenate(both, axis=1).astype(F32).T.astype(BF16))
    for t in range(0, count, 2):
        total = None
        for q_ref, side in zip(q_refs, sides):
            pair = jnp.concatenate([q_ref[t], q_ref[t + 1]], axis=1)
            part = dot(side, pair)
            total = part if total is None else total + part
        for k in range(2):
            block = total[:, k * width : (k + 1) * width]
            for n, out_ref in enumerate(out_refs):
                share = block[n * width : (n + 1) * width]
                out_ref[t + k] = share + before[n][t + k] if more else share


def final_kernel(
    pos_ref,
    rank_ref,
    listed_ref,
    row_rank_ref,
    col_rank_ref,
    u_hbm,
    v_hbm,
    uu_ref,
    own_ref,
    other_ref,
    vproj_ref,
    st_ref,
    *refs,
    masks,
    block,
    pieces,
):
    x_refs, refs = refs[:pieces], refs[pieces:]
    panel_refs, refs = refs[: 2 * len(masks)], refs[2 * len(masks) :]
    (
        out_u,
        out_v,
        u_buf,
        v_buf,
        left_buf,
        x_buf,
        to_u,
        to_v,
        gs,
        rs,
        ts,
        scales,
        mixes,
        to_mix,
        to_coef,
        sem_u,
        sem_v,
        sem_out,
    ) = refs
    count, order, width = u_hbm.shape
    chunk = panel_refs[0].shape[1]
    depth = x_refs[0].shape[1]
    def rows_at(k):
        start = jnp.bitwise_xor(pos_ref[1], masks[k // 2] + k % 2) * chunk
        return pl.ds(pl.multiple_of(start, chunk), chunk)

    spans = [pl.ds(k * chunk, chunk) for k in range(len(panel_refs))]
    loads = [
        pltpu.make_async_copy(u_hbm.at[:, rows_at(k), :], u_buf.at[:, span, :], sem_u.at[k])
        for k, span in enumerate(spans)
    ]
    for copy in loads:
        copy.start()
    load_v = pltpu.make_async_copy(v_hbm, v_buf, sem_v)
    load_v.start()
    for k in range(pieces):
        start = lax.rem(pos_ref[0] + pieces - k, pieces) * depth
        rows = pl.ds(pl.multiple_of(start, depth), depth)
        x_buf[rows, :] = x_refs[k][0]

    def send_u(t, k):
        src = to_u.at[t, spans[k], :]
        return pltpu.make_async_copy(src, out_u.at[t, rows_at(k), :], sem_out.at[0])

    def send_v(t):
        return pltpu.make_async_copy(to_v.at[t], out_v.at[t], sem_out.at[1])

    square = (width, width)
    eye = rows_of(square) == lanes(square)
    xproj = dot(st_ref[...], x_buf[...])
    xproj = jnp.where(lanes(square) < col_rank_ref[0], -xproj, 0.0).astype(BF16)

    for t in range(count):
        core = own_ref[t] + other_ref[t]
        keep = (lanes(square) < row_rank_ref[t]) & (rows_of(square) < col_rank_ref[0])
        core = jnp.where(keep, core, 0.0).astype(BF16)
        panel = jnp.concatenate([ref[t] for ref in panel_refs], axis=0)
        left_buf[t] = dot(panel, core, 1, 1).astype(BF16)
    for copy in loads:
        copy.wait()

    for t in range(count):
        left = left_buf[t]
        ts[t] = dot(left, jnp.concatenate([u_buf[t], left], axis=1), 0, 0)
    b = xproj
    for t in range(count):
        low = ts[t]
        lu_h, lu_l = halves(low[:, :width])
        ll_h, ll_l = halves(low[:, width:])
        uu_h, uu_l = halves(uu_ref[t])
        a = vproj_ref[t]
        left_part = dot(a, uu_h) + dot(a, uu_l) + dot(b, lu_h) + dot(b, lu_l)
        right_part = dot(a, lu_h, 1, 1) + dot(a, lu_l, 1, 1) + dot(b, ll_h) + dot(b, ll_l)
        ts[t] = jnp.concatenate([left_part, right_part], axis=1)
    for t in range(count):
        moved_h, moved_l = halves(ts[t])
        weights = jnp.concatenate([vproj_ref[t], b], axis=1)
        gs[pl.ds(t * width, width), :] = dot(moved_h, weights, 1, 1) + dot(moved_l, weights, 1, 1)
    for t in range(count):
        at = pl.ds(t * width, width)
        gram = gs[at, :]
        diag = jnp.where(eye, gram, 0.0)
        trace = jnp.sum(jnp.sum(diag, axis=1, keepdims=True), axis=0, keepdims=True)
        scale = trace / width + 0.0001
        gs[at, :] = gram * (1.0 / scale) + jnp.where(eye, 0.01, 0.0)
        scales[t] = jnp.broadcast_to(lax.rsqrt(scale), scales.shape[1:])

    lane = lanes((count, width))
    small = 8
    for k0 in range(0, width, block):
        end = k0 + block
        taken = jnp.stack([gs[pl.ds(n * width + k0, block), :] for n in range(count)])
        taken = jnp.swapaxes(taken, 0, 1)
        rows = [taken[r] for r in range(block)]
        ready = []
        for b0 in range(0, block, small):
            first = k0 + b0
            inside = (lane >= first) & (lane < first + small)
            part = rows[b0 : b0 + small]
            a = [
                [part[i][:, first + j : first + j + 1] for j in range(i + 1)]
                for i in range(small)
            ]
            a = [[jnp.broadcast_to(x, (count, width)) for x in line] for line in a]
            part = [
                jnp.where(inside, jnp.where(lane == first + i, 1.0, 0.0), x)
                for i, x in enumerate(part)
            ]
            for j in range(small):
                root = lax.rsqrt(a[j][j])
                part[j] = part[j] * root
                factors = {i: a[i][j] * root for i in range(j + 1, small)}
                for i in range(j + 1, small):
                    for m in range(j + 1, i + 1):
                        a[i][m] = a[i][m] - factors[i] * factors[m]
                    part[i] = part[i] - factors[i] * part[j]
            for r in range(b0 + small, block):
                row = jnp.where(inside, 0.0, rows[r])
                for j in range(small):
                    row = row - part[j][:, k0 + r : k0 + r + 1] * part[j]
                rows[r] = row
            ready += part
        ready = jnp.swapaxes(jnp.stack(ready), 0, 1)
        for n in range(count):
            rs[pl.ds(n * width + k0, block), :] = ready[n]
        if end < width:
            strip = (block, width)
            strip_lane = lanes(strip)
            own = k0 + rows_of(strip)
            group = min(count, width // block)
            ahead, use = [], []
            for n in range(count):
                done = ready[n]
                ahead.append(jnp.where(strip_lane >= end, done, 0.0))
                use.append(jnp.where((strip_lane > own) & (strip_lane < end), 0.0, done))
            changes = []
            for g in range(0, count, group):
                a_h, a_l = halves(jnp.concatenate(ahead[g : g + group], axis=0).T[end:])
                both = jnp.concatenate([a_h, a_l], axis=1)
                for n in range(0, group, 2):
                    cells = []
                    for m in (n, n + 1):
                        spread = [jnp.zeros(strip, F32)] * group
                        spread[m] = use[g + m]
                        cells.append(jnp.concatenate(spread, axis=0))
                    b_h, b_l = halves(jnp.concatenate(cells, axis=1))
                    change = dot(both, jnp.concatenate([b_h, b_h], axis=0)) + dot(a_h, b_l)
                    changes += [change[:, :width], change[:, width:]]
            for n in range(count):
                rest = pl.ds(n * width + end, width - end)
                old = gs[rest, :]
                gone = lanes(old.shape)
                gs[rest, :] = jnp.where((gone >= k0) & (gone < end), 0.0, old) - changes[n]

    for t in range(count):
        at = pl.ds(t * width, width)
        inverse = jnp.where(lanes(square) <= rows_of(square), rs[at, :], 0.0)
        rs[at, :] = inverse * (scales[t][:1, :1] * (float(order) ** 0.5))
    for t in range(count):
        inv_h, inv_l = halves(rs[pl.ds(t * width, width), :])
        weights = jnp.concatenate([vproj_ref[t], b], axis=1)
        mixes[t] = dot(inv_h, weights) + dot(inv_l, weights)
        moved_h, moved_l = halves(ts[t])
        ts[t] = dot(inv_h, moved_h) + dot(inv_h, moved_l) + dot(inv_l, moved_h)
    for t in range(count):
        tile_rank = rank_ref[t]
        picked = listed_ref[t] == 1
        mixed_h, mixed_l = halves(mixes[t])
        coef = ts[t]
        coef = coef * (1.0 / order)
        wide = coef.shape
        col = lanes(wide)
        row = rows_of(wide)
        in_u = col < width
        keep = (col == row) & (col < tile_rank)
        moved_to = (col >= width) & (row == col - width + tile_rank)
        exact_u = jnp.where(keep | moved_to, 1.0, 0.0)
        moved_to = moved_to & (col - width < col_rank_ref[0])
        exact_v = jnp.where(keep, 1.0, jnp.where(moved_to, -1.0, 0.0))
        coef = jnp.where(in_u, jnp.where(col < tile_rank, coef, 0.0), -coef)
        coef = jnp.where(picked, coef, exact_v).astype(BF16)
        mixed_h = jnp.where(picked, mixed_h.astype(F32), exact_u).astype(BF16)
        mixed_l = jnp.where(picked, mixed_l.astype(F32), 0.0).astype(BF16)
        both = jnp.concatenate([mixed_h, mixed_l], axis=0)
        to_mix[t] = both
        to_coef[t] = coef

    load_v.wait()

    def finish(t):
        side = jnp.concatenate([u_buf[t], left_buf[t]], axis=1)
        result = dot(side, to_mix[t], 1, 1)
        to_u[t] = (result[:, :width] + result[:, width:]).astype(BF16)
        for k in range(len(spans)):
            send_u(t, k).start()
        side = jnp.concatenate([v_buf[t], x_buf[...]], axis=1)
        to_v[t] = dot(side, to_coef[t], 1, 1).astype(BF16)
        send_v(t).start()

    for t in range(count):
        finish(t)
    pltpu.make_async_copy(to_u, out_u, sem_out.at[0]).wait()
    pltpu.make_async_copy(to_v, out_v, sem_out.at[1]).wait()


def swap(x, axis, size, mask):
    return lax.ppermute(x, axis, [(c, c ^ mask) for c in range(size)])


def on_device(
    n_row,
    n_col,
    tile_u,
    tile_v,
    tile_rank,
    listed,
    row_u,
    row_v,
    row_rank,
    col_u,
    col_v,
    col_rank,
    sketch,
):
    rows_here, cols_here, order, width = tile_u.shape
    assert cols_here == 1 and width == sketch.shape[1]
    count = rows_here * cols_here
    chunk = row_u.shape[1]
    tile_u = tile_u.reshape(count, order, width)
    tile_v = tile_v.reshape(count, order, width)
    tile_rank = tile_rank.reshape(count)
    listed = listed.reshape(count)
    pos = jnp.stack([lax.axis_index("row"), lax.axis_index("col")]).astype(jnp.int32)
    col_swap = lambda x, mask: swap(x, "col", n_col, mask)
    dims = []
    mask = 2
    while mask < n_col:
        dims.append(mask)
        mask *= 2

    tie = lax.optimization_barrier

    def gather(own, order, found):
        for m in order:
            for r in sorted(found):
                if not r & m and r | m not in found:
                    found[r | m] = col_swap(found[r], m)
        return found

    def shift(v, step):
        return lax.ppermute(v, "row", [(c, (c + step) % n_row) for c in range(n_row)])

    q = {0: row_v, **{m: col_swap(row_v, m) for m in dims}}
    p = {0: row_u, **{m: col_swap(row_u, m) for m in dims}}
    y = [col_v]
    for _ in range(n_row - 2):
        y.append(shift(y[-1], 1))
    cost = pl.CostEstimate(
        flops=2 * count * order * width * width,
        bytes_accessed=2 * count * order * width,
        transcendentals=0,
    )
    uu = pl.pallas_call(
        gram_kernel,
        in_specs=[VMEM],
        out_specs=VMEM,
        out_shape=jax.ShapeDtypeStruct((count, width, width), F32),
        compiler_params=pltpu.CompilerParams(vmem_limit_bytes=16 * MIB),
        cost_estimate=cost,
        name="gram_products",
    )(tile_u)
    y[-1], x_own, q[dims[0]], p[dims[-1]], uu = tie(
        (y[-1], col_u, q[dims[0]], p[dims[-1]], uu)
    )
    y.append(shift(y[-1], 1))
    x = [x_own, shift(x_own, 1)]
    q, p, x, tile_v, sketch = tie((q, p, x, tile_v, sketch))
    turned = sketch.T
    vproj = pl.pallas_call(
        proj_kernel,
        in_specs=[SMEM, VMEM, VMEM],
        out_specs=VMEM,
        out_shape=jax.ShapeDtypeStruct((count, width, width), BF16),
        compiler_params=pltpu.CompilerParams(vmem_limit_bytes=16 * MIB),
        cost_estimate=cost,
        name="sketch_products",
    )(tile_rank, turned, tile_v)
    back = shift(x[0], -1)
    for _ in range(n_row - 3):
        x.append(shift(x[-1], 1))
    x.append(back)
    q = gather(row_v, dims, q)
    p = gather(row_u, dims[::-1], p)
    y_other = col_swap(jnp.concatenate(y, axis=0), 1)
    own_mate = col_swap(row_u, 1)
    masks = tuple(range(0, n_col, 2))
    part_shape = jax.ShapeDtypeStruct((count, width, width), F32)

    def cores(use, before, outs=(0, 1)):
        return pl.pallas_call(
            functools.partial(
                core_kernel, masks=use, pieces=n_row, more=len(before) > 0, outs=outs
            ),
            in_specs=[SMEM] + [VMEM] * (len(use) + n_row + 1 + len(before)),
            out_specs=[VMEM] * len(outs),
            out_shape=[part_shape] * len(outs),
            compiler_params=pltpu.CompilerParams(vmem_limit_bytes=16 * MIB),
            cost_estimate=pl.CostEstimate(
                flops=4 * len(use) * count * chunk * width * width,
                bytes_accessed=2 * len(use) * count * chunk * width,
                transcendentals=0,
            ),
            name="core_products",
        )(pos, *[q[m] for m in use], *y, y_other, *before)

    parts = cores(masks[:-1], []) if len(masks) > 1 else []
    parts, x, vproj = tie((parts, x, vproj))
    (core_other,) = cores(masks[-1:], parts[1:], (1,))
    core_got = col_swap(core_other, 1)
    (core_own,) = cores(masks[-1:], parts[:1], (0,))

    panels = [row_u, own_mate]
    for m in masks[1:]:
        panels += [p[m], col_swap(p[m], 1)]
    out_shape = jax.ShapeDtypeStruct((count, order, width), BF16)
    out_u, out_v = pl.pallas_call(
        functools.partial(
            final_kernel,
            masks=masks,
            block=32,
            pieces=n_row,
        ),
        in_specs=[SMEM] * 5 + [HBM] * 2 + [VMEM] * (5 + n_row + len(panels)),
        out_specs=[HBM, HBM],
        out_shape=[out_shape, out_shape],
        scratch_shapes=[
            pltpu.VMEM((count, order, width), BF16),
            pltpu.VMEM((count, order, width), BF16),
            pltpu.VMEM((count, order, width), BF16),
            pltpu.VMEM((order, width), BF16),
            pltpu.VMEM((count, order, width), BF16),
            pltpu.VMEM((count, order, width), BF16),
            pltpu.VMEM((count * width, width), F32),
            pltpu.VMEM((count * width, width), F32),
            pltpu.VMEM((count, width, 2 * width), F32),
            pltpu.VMEM((count, 8, width), F32),
            pltpu.VMEM((count, width, 2 * width), F32),
            pltpu.VMEM((count, 2 * width, 2 * width), BF16),
            pltpu.VMEM((count, width, 2 * width), BF16),
            pltpu.SemaphoreType.DMA((len(panels),)),
            pltpu.SemaphoreType.DMA,
            pltpu.SemaphoreType.DMA((2,)),
        ],
        compiler_params=pltpu.CompilerParams(vmem_limit_bytes=40 * MIB),
        cost_estimate=pl.CostEstimate(
            flops=16 * count * order * width * width,
            bytes_accessed=10 * count * order * width,
            transcendentals=0,
        ),
        name="recompress_store",
    )(
        pos,
        tile_rank,
        listed,
        row_rank,
        col_rank,
        tile_u,
        tile_v,
        uu,
        core_own,
        core_got,
        vproj,
        turned,
        *x,
        *panels,
    )
    shape = (rows_here, cols_here, order, width)
    return out_u.reshape(shape), out_v.reshape(shape)


def solution(mesh):
    return jax.shard_map(
        functools.partial(on_device, mesh.shape["row"], mesh.shape["col"]),
        mesh=mesh,
        in_specs=(
            P("row", "col", None, None),
            P("row", "col", None, None),
            P("row", "col"),
            P("row", "col"),
            P("row", "col", None),
            P("row", "col", None),
            P("row"),
            P("col", "row", None),
            P("col", "row", None),
            P("col"),
            P(),
        ),
        out_specs=(P("row", "col", None, None), P("row", "col", None, None)),
        check_vma=False,
    )
```
